128 devices in a mesh: rcv: 8 (over z_hi, y), src: 16 (over z_lo, x, core).
Axes of the slice: x: 4, y: 4, z: 4 (z_hi: 2, z_lo: 2; z = z_hi * 2 + z_lo), core: 2. Of those that a mesh axis runs over, the one named last changes fastest.
Arguments:
- kernel: bfloat16 [6912, 110592], P('rcv', 'src'), may hold values from -0.02734375 to 0.02734375
- rates: float32 [110592, 256], P(('rcv', 'src')), may hold values from 0.1 to 10
- state: float32 [6912, 256], P(('rcv', 'src')), may hold values from 0.1 to 10
- a_sigma: float32 [6912, 256], P(('rcv', 'src')), may hold values from 0.5 to 2
- b_sigma: float32 [6912, 256], P(('rcv', 'src')), may hold values from 0.5 to 2.5
- slip_distance: float32 [6912, 256], P(('rcv', 'src')), may hold values from 0.2 to 5
Outputs:
- rate_change: float32 [6912, 256], P(('rcv', 'src'))
- state_change: float32 [6912, 256], P(('rcv', 'src'))
The draws below stay inside these ranges and needn't reach their ends.
All inputs are finite; a program needn't handle non-finite values.
Results may differ from the reference program's by a relative error of at most 0.0033.
Values may be sent and summed in bfloat16 or wider, within the bound.
A program may use at most 192 MiB of HBM per device.

```python
import math
import jax
import jax.numpy as jnp
from jax import lax

MEMBERS = 256
NS = 110592
NR = 6912


def spiked(entries, key, source, target, shards_of, factor):
    def block_of(dim):
        return (jnp.arange(entries.shape[dim]) // (entries.shape[dim] // shards_of)).reshape((-1,) + (1,) * (entries.ndim - 1 - dim))

    one_side = jax.random.permutation(key, shards_of)[block_of(target)]
    other_side = (block_of(target) + shards_of // 2) % shards_of
    return jnp.where((block_of(source) == one_side) | (block_of(source) == other_side), factor * entries, entries)


def block_levels(key, extent, shards, smallest, largest):
    gain = 1.0
    for axis_at, parts in shards:
        draws = jax.random.uniform(jax.random.fold_in(jax.random.fold_in(key, 6), axis_at), (parts,), jnp.float32, smallest / len(shards), largest / len(shards))
        gain = gain * jnp.repeat(jnp.exp(draws), extent[axis_at] // parts).reshape((-1,) + (1,) * (len(extent) - 1 - axis_at))
    return gain


def bell_draw_with(rng, dims, spread, bound, shards, heavy, dtype=jnp.bfloat16):
    drawn = spread * jax.random.normal(rng, dims, jnp.float32)
    if shards:
        drawn = drawn * block_levels(rng, dims, shards, -0.22, 0.18)
    return jnp.clip(spiked(drawn, jax.random.fold_in(rng, 3), *heavy), -bound, bound).astype(dtype)


def setup_inputs(seed: int = 0) -> dict:
    arg_keys = jax.random.split(jax.random.key(seed), 7)
    kernel = bell_draw_with(arg_keys[0], (NR, NS), NS ** -0.5, 0.02734375, ((0, 8), (1, 16)), (1, 0, 16, 2.0))
    rates = jnp.clip(jnp.exp(math.log(10.0) - 4.6051702 * jax.random.uniform(arg_keys[1], (NS, MEMBERS), jnp.float32) ** block_levels(arg_keys[1], (NS, MEMBERS), ((0, 128),), -0.2, 0.2)), 0.1, 10.0)
    state = jnp.clip(jnp.exp(math.log(10.0) - 4.6051702 * jax.random.uniform(arg_keys[2], (NR, MEMBERS), jnp.float32) ** block_levels(arg_keys[2], (NR, MEMBERS), ((0, 128),), -0.2, 0.2)), 0.1, 10.0)
    a_sigma = jnp.clip(jnp.exp(math.log(2.0) - 1.3862944 * jax.random.uniform(arg_keys[3], (NR, MEMBERS), jnp.float32) ** block_levels(arg_keys[3], (NR, MEMBERS), ((0, 128),), -0.2, 0.2)), 0.5, 2.0)
    b_sigma = jnp.clip(jnp.exp(math.log(2.5) - 1.609438 * jax.random.uniform(arg_keys[4], (NR, MEMBERS), jnp.float32) ** block_levels(arg_keys[4], (NR, MEMBERS), ((0, 128),), -0.2, 0.2)), 0.5, 2.5)
    slip_distance = jnp.clip(jnp.exp(math.log(5.0) - 3.218876 * jax.random.uniform(arg_keys[5], (NR, MEMBERS), jnp.float32) ** block_levels(arg_keys[5], (NR, MEMBERS), ((0, 128),), -0.2, 0.2)), 0.2, 5.0)
    return dict(kernel=kernel, rates=rates, state=state, a_sigma=a_sigma, b_sigma=b_sigma, slip_distance=slip_distance)


damping = 0.5


def reference(kernel, rates, state, a_sigma, b_sigma, slip_distance):
    deficit = (rates - 1.0).astype(jnp.bfloat16)
    blocks = kernel.reshape(16, NR // 16, NS)

    def row_block(block_rows):
        return jnp.dot(block_rows, deficit, preferred_element_type=jnp.float32)

    stress = lax.map(row_block, blocks).reshape(NR, MEMBERS)
    own_rate = deficit[:NR].astype(jnp.float32) + 1.0
    state_change = 1.0 - own_rate * state / slip_distance
    rate_change = (stress - b_sigma / state * state_change) / (a_sigma / own_rate + damping)
    return rate_change, state_change
```

```python
import functools

import jax
import jax.numpy as jnp
from jax import lax
from jax.experimental import pallas as pl
from jax.experimental.pallas import tpu as pltpu
from jax.sharding import PartitionSpec as P

damping = 0.5
MESH = pl.DeviceIdType.MESH
LANES = 128


def gather_and_multiply(
    pr, qr, qc, kernel_ref, rates_ref, stress_ref, own_ref,
    kv, rv, pbuf, qbuf, dbuf, acc, sb, cb, rb, ob, od,
    k_sem, r_sem, pz_r, py_r, px_r, qy_r, d_r, rs_r, cx_r, od_r,
    pa_s, pb_s, py_s, px_s, qy_s, qx_s, qa_s, qb_s, cx_s, rs_s, od_s,
):
    r = lax.axis_index("rcv")
    s = lax.axis_index("src")
    y = lax.rem(r, 4)
    z = 2 * lax.div(r, 4) + lax.div(s, 8)
    x = lax.div(lax.rem(s, 8), 2)
    c = lax.rem(s, 2)
    zp = lax.rem(z, 2)
    p = 2 * x + c
    rows = pr + qr
    nq = qr // qc

    def m4(v):
        return lax.rem(v + 8, 4)

    def dev(dx, dy, dz, dc):
        return (4 * lax.div(dz, 2) + dy, 8 * lax.rem(dz, 2) + 2 * dx + dc)

    outer = (z == 0) | (z == 3)
    inner = jnp.logical_not(outer)
    home_core = c == zp
    owner = outer & home_core
    mid = inner & home_core
    relay = outer & jnp.logical_not(home_core)
    inner_i = jnp.where(inner, 1, 0)
    za = 3 * (1 - zp)
    zb = 1 + zp
    kk = jnp.where(z < 2, 1, 0)
    own_slot = jnp.where(outer, 2 * y + (1 - kk), 8)

    k_copy = pltpu.make_async_copy(kernel_ref, kv, k_sem)
    r_copy = pltpu.make_async_copy(rates_ref, rv, r_sem)
    r_copy.start()
    k_copy.start()

    bar = pltpu.get_barrier_semaphore()
    friends = [dev(x, m4(y + 1), z, c), dev(x, m4(y - 1), z, c), dev(x, y, m4(z + 1), c), dev(x, y, m4(z - 1), c)]
    friends += [dev(m4(x + d), y, z, 1 - c if k else c) for d in range(4) for k in range(2) if d or k]
    zx = z + 1 - 2 * zp
    friends += [dev(m4(x + d), y, zx, c) for d in range(1, 4)]
    for f in friends:
        pl.semaphore_signal(bar, inc=1, device_id=f, device_id_type=MESH)
    gives_own = (r == 0) & (s < 8)

    @pl.when(jnp.logical_not((r == 0) & (s == 0)))
    def _():
        pl.semaphore_signal(bar, inc=1, device_id=(0, r), device_id_type=MESH)

    r_copy.wait()
    for h in range(2):
        cols = slice(LANES * h, LANES * (h + 1))
        pbuf[h, own_slot] = (rv[:pr, cols] - 1.0).astype(jnp.bfloat16)
        qbuf[h, y] = (rv[pr:, cols] - 1.0).astype(jnp.bfloat16)

    pl.semaphore_wait(bar, len(friends) + jnp.where(gives_own, jnp.where(s == 0, 15, 16), 0))

    def remote(src, dst, ssem, rsem, to):
        return pltpu.make_async_remote_copy(
            src_ref=src, dst_ref=dst, send_sem=ssem, recv_sem=rsem, device_id=to, device_id_type=MESH
        )

    def landed(dst, sem):
        pltpu.make_async_copy(dst, dst, sem).wait()

    def qrows(piece, j):
        return pl.ds(pl.multiple_of(piece * rows + pr + j * qc, 16), qc)

    def prows(piece):
        return pl.ds(pl.multiple_of(piece * rows, 16), pr)

    def send_pa(h):
        dst = jnp.where(outer, 8, 2 * y + kk)
        sem = jnp.where(outer, 2, kk)
        remote(pbuf.at[h, own_slot], pbuf.at[h, dst], pa_s.at[h], pz_r.at[h, sem], dev(x, y, za, c)).start()

    def send_pb(h):
        remote(pbuf.at[h, 8], pbuf.at[h, 2 * y + kk], pb_s.at[h], pz_r.at[h, kk], dev(x, y, zb, c)).start()

    def send_py(h, e, k, way):
        slot = 2 * m4(y + e) + k
        to_e = (e - way) % 4 - 1
        remote(pbuf.at[h, slot], pbuf.at[h, slot], py_s.at[h], py_r.at[h, to_e, k], dev(x, m4(y + way), z, c)).start()

    def wait_py(h, e, k):
        landed(pbuf.at[h, 2 * m4(y + e) + k], py_r.at[h, (e % 4) - 1, k])

    def send_qy(h, e, j, way):
        part = qbuf.at[h, m4(y + e), pl.ds(j * qc, qc)]
        to_e = (e - way) % 4 - 1
        remote(part, part, qy_s.at[h], qy_r.at[h, to_e, j], dev(x, m4(y + way), z, c)).start()

    def wait_qy(h, e, j):
        landed(qbuf.at[h, m4(y + e), pl.ds(j * qc, qc)], qy_r.at[h, (e % 4) - 1, j])

    def send_px(h, e):
        to_x = m4(y + e)
        dst = dbuf.at[0, h, prows(p)]
        for k in range(2):
            core = 1 - c if k else c
            src = pbuf.at[h, 2 * to_x + core]
            there = remote(src, dst, px_s.at[h], px_r.at[h, p], dev(to_x, y, z, core))
            if k:
                there.start()
            else:
                pl.when(to_x != x)(there.start)
                here = pltpu.make_async_copy(src, dst, px_r.at[h, p])
                pl.when(to_x == x)(here.start)

    def send_qx(h, e, j):
        to_x = m4(y + e)
        src = qbuf.at[h, to_x, pl.ds(j * qc, qc)]
        dst = dbuf.at[inner_i, h, qrows(p, j)]
        sem = d_r.at[inner_i, h, p, j]
        me = (to_x == x) & home_core
        there = remote(src, dst, qx_s.at[h], sem, dev(to_x, y, z, zp))
        here = pltpu.make_async_copy(src, dst, sem)
        pl.when(jnp.logical_not(me))(there.start)
        pl.when(me)(here.start)

    def pass_z(h, piece, j):
        part = qrows(piece, j)
        final = dbuf.at[0, h, part]
        spare = dbuf.at[1, h, part]
        f_sem = d_r.at[0, h, piece, j]
        s_sem = d_r.at[1, h, piece, j]

        @pl.when(owner)
        def _():
            landed(final, f_sem)
            remote(final, spare, qa_s.at[h], s_sem, dev(x, y, za, c)).start()

        @pl.when(mid)
        def _():
            landed(spare, s_sem)
            remote(spare, final, qa_s.at[h], f_sem, dev(x, y, za, c)).start()
            remote(spare, final, qb_s.at[h], f_sem, dev(x, y, zb, c)).start()

        @pl.when(relay)
        def _():
            landed(spare, s_sem)
            remote(spare, final, qb_s.at[h], f_sem, dev(x, y, zb, c)).start()

    def start(h):
        send_pa(h)
        pl.when(inner)(functools.partial(send_pb, h))
        for j in range(nq):
            send_qy(h, 0, j, 1)
            send_qy(h, 0, j, -1)
        for j in range(nq):
            send_qx(h, 0, j)

    def q_ring(h):
        for j in range(nq):
            wait_qy(h, -1, j)
            if j % 2 == 0:
                send_qy(h, -1, j, 1)
            wait_qy(h, 1, j)
            if j % 2 == 1:
                send_qy(h, 1, j, -1)
            send_qx(h, -1, j)
            send_qx(h, 1, j)

    def q_far(h):
        for j in range(nq):
            wait_qy(h, 2, j)
            send_qx(h, 2, j)

    def p_relay(h):
        @pl.when(outer)
        def _():
            landed(pbuf.at[h, 8], pz_r.at[h, 2])
            send_pb(h)

    def p_slots(h):
        landed(pbuf.at[h, 2 * y + kk], pz_r.at[h, kk])

        @pl.when(inner)
        def _():
            landed(pbuf.at[h, 2 * y + 1 - kk], pz_r.at[h, 1 - kk])

        for k in range(2):
            send_py(h, 0, k, 1)
            send_py(h, 0, k, -1)
        send_px(h, 0)

    def p_ring(h):
        for k in range(2):
            wait_py(h, -1, k)
            if k == 0:
                send_py(h, -1, k, 1)
            wait_py(h, 1, k)
            if k == 1:
                send_py(h, 1, k, -1)
        send_px(h, -1)
        send_px(h, 1)

    def p_far(h):
        wait_py(h, 2, 0)
        wait_py(h, 2, 1)
        send_px(h, 2)

    def z_pass(h):
        for d in (0, 1, 3, 2):
            for cc in range(2):
                for j in range(nq):
                    pass_z(h, 2 * m4(x + d) + cc, j)

    depth = 768
    steps = kv.shape[1] // depth

    def product(h):
        for i in range(steps):
            if i < 8:
                landed(dbuf.at[0, h, prows(i)], px_r.at[h, i])

                @pl.when(jnp.logical_not(owner))
                def _():
                    for j in range(nq):
                        landed(dbuf.at[0, h, qrows(i, j)], d_r.at[0, h, i, j])

            part = jnp.dot(
                kv[:, i * depth:(i + 1) * depth], dbuf[0, h, i * depth:(i + 1) * depth],
                preferred_element_type=jnp.float32,
            )
            if i == 0:
                acc[...] = part
            else:
                acc[...] += part

    rec = rows // 16

    def sum_start(h):
        for b in range(16):
            sb[h, b % 2, b // 2, :rec] = acc[b * rec:(b + 1) * rec]
        remote(sb.at[h, 1 - c], cb.at[h], cx_s.at[h], cx_r.at[h], dev(x, y, z, 1 - c)).start()

    def sum_cores(h):
        landed(cb.at[h], cx_r.at[h])
        sb[h, c] = sb[h, c] + cb[h]
        for n in range(1, 8):
            to_x = m4(x + n % 4)
            to_z = zx if n >= 4 else z
            block = 4 * lax.rem(to_z, 2) + to_x
            remote(sb.at[h, c, block], rb.at[h, n], rs_s.at[h], rs_r.at[h, n], dev(to_x, y, to_z, c)).start()

    def sum_end(h):
        total = sb[h, c, 4 * zp + x]
        for n in range(1, 8):
            landed(rb.at[h, n], rs_r.at[h, n])
            total = total + rb[h, n]
        stress_ref[:, LANES * h:LANES * (h + 1)] = total[:rec]

    start(0)
    start(1)

    @pl.when(gives_own)
    def _():
        for b in range(16):
            ob[b, :rec] = (rv[b * rec:(b + 1) * rec] - 1.0).astype(jnp.bfloat16)
            there = remote(ob.at[b], od, od_s, od_r, (s, b))
            if b:
                there.start()
            else:
                pl.when(s != 0)(there.start)
                pl.when(s == 0)(pltpu.make_async_copy(ob.at[b], od, od_r).start)

    q_ring(0)
    p_relay(0)
    p_slots(0)
    q_far(0)
    q_ring(1)
    p_relay(1)
    p_ring(0)
    p_slots(1)
    z_pass(0)
    p_far(0)
    q_far(1)
    p_ring(1)
    p_far(1)
    k_copy.wait()
    z_pass(1)
    product(0)
    sum_start(0)
    sum_cores(0)
    product(1)
    sum_start(1)
    sum_cores(1)
    landed(od, od_r)
    own_ref[...] = od[:rec].astype(jnp.float32)
    sum_end(0)
    sum_end(1)

    def sent(sem, like, n=1):
        ref = like if n == 1 else like.at[pl.ds(0, n)]
        pltpu.make_async_copy(ref, ref, sem).wait()

    for h in range(2):
        sent(pa_s.at[h], pbuf.at[h, 0])
        sent(pb_s.at[h], pbuf.at[h, 0])
        sent(py_s.at[h], pbuf.at[h, pl.ds(0, 6)])
        sent(px_s.at[h], pbuf.at[h, pl.ds(0, 7)])
        sent(qy_s.at[h], qbuf.at[h, pl.ds(0, 3)])

        @pl.when(home_core)
        def _():
            sent(qx_s.at[h], qbuf.at[h, pl.ds(0, 3)])
            sent(qa_s.at[h], dbuf.at[0, h, pl.ds(0, 8 * qr)])

        @pl.when(jnp.logical_not(home_core))
        def _():
            sent(qx_s.at[h], qbuf.at[h, pl.ds(0, 4)])

        @pl.when(mid | relay)
        def _():
            sent(qb_s.at[h], dbuf.at[0, h, pl.ds(0, 8 * qr)])

        sent(cx_s.at[h], sb.at[h, 0])
        sent(rs_s.at[h], sb.at[h, 0, pl.ds(0, 7)])

    @pl.when(gives_own & (s != 0))
    def _():
        sent(od_s, ob)

    @pl.when(gives_own & (s == 0))
    def _():
        sent(od_s, ob.at[pl.ds(0, 15)])


def per_device(kernel, rates, state, a_sigma, b_sigma, slip_distance):
    patches, members = rates.shape
    rec_rows = state.shape[0]
    pr = 352
    qr = patches - pr
    qc = qr // 2
    nq = 2
    bf16, f32 = jnp.bfloat16, jnp.float32
    dma = pltpu.SemaphoreType.DMA
    rec_pad = -(-rec_rows // 8) * 8
    stress, own_deficit = pl.pallas_call(
        functools.partial(gather_and_multiply, pr, qr, qc),
        out_shape=[jax.ShapeDtypeStruct((rec_rows, members), f32)] * 2,
        in_specs=[pl.BlockSpec(memory_space=pl.ANY)] * 2,
        out_specs=[pl.BlockSpec(memory_space=pltpu.VMEM)] * 2,
        scratch_shapes=[
            pltpu.VMEM(kernel.shape, bf16),
            pltpu.VMEM(rates.shape, f32),
            pltpu.VMEM((2, 9, pr, LANES), bf16),
            pltpu.VMEM((2, 4, qr, LANES), bf16),
            pltpu.VMEM((2, 2, 8 * patches, LANES), bf16),
            pltpu.VMEM((patches, LANES), f32),
            pltpu.VMEM((2, 2, 8, rec_pad, LANES), f32),
            pltpu.VMEM((2, 8, rec_pad, LANES), f32),
            pltpu.VMEM((2, 8, rec_pad, LANES), f32),
            pltpu.VMEM((16, 64, members), bf16),
            pltpu.VMEM((64, members), bf16),
            dma, dma,
            dma((2, 3)), dma((2, 3, 2)), dma((2, 8)), dma((2, 3, nq)), dma((2, 2, 8, nq)),
            dma((2, 8)), dma((2,)), dma,
            dma((2,)), dma((2,)), dma((2,)), dma((2,)), dma((2,)), dma((2,)), dma((2,)), dma((2,)),
            dma((2,)), dma((2,)), dma,
        ],
        compiler_params=pltpu.CompilerParams(
            collective_id=0, has_side_effects=True, vmem_limit_bytes=48 * 2**20
        ),
        cost_estimate=pl.CostEstimate(
            flops=2 * kernel.size * members, bytes_accessed=kernel.size * 2 + rates.size * 4, transcendentals=0
        ),
    )(kernel, rates)
    own_rate = own_deficit + 1.0
    state_change = 1.0 - own_rate * state / slip_distance
    rate_change = (stress - b_sigma / state * state_change) / (a_sigma / own_rate + damping)
    return (rate_change, state_change)


def solution(mesh):
    rows = P(("rcv", "src"), None)
    return jax.shard_map(
        per_device, mesh=mesh, in_specs=(P("rcv", "src"), rows, rows, rows, rows, rows),
        out_specs=(rows, rows), check_vma=False,
    )
```

```python
import functools

import jax
import jax.numpy as jnp
from jax import lax
from jax.experimental import pallas as pl
from jax.experimental.pallas import tpu as pltpu
from jax.sharding import PartitionSpec as P

damping = 0.5
MESH = pl.DeviceIdType.MESH
LANES = 128
GROUPS = 3
CHUNKS = 2 * GROUPS


def gather_and_multiply(
    pc, qc, kernel_ref, rates_ref, stress_ref, own_ref,
    kv, kp, kq, rv, pbuf, qbuf, dp, dq, acc, sb, cb, rb, ob, od,
    k_sem, r_sem, pz_r, py_r, px_r, qy_r, d_r, rs_r, cx_r, od_r,
    pa_s, pb_s, py_s, px_s, qy_s, qx_s, qa_s, qb_s, cx_s, rs_s, od_s,
):
    r = lax.axis_index("rcv")
    s = lax.axis_index("src")
    y = lax.rem(r, 4)
    z = 2 * lax.div(r, 4) + lax.div(s, 8)
    x = lax.div(lax.rem(s, 8), 2)
    c = lax.rem(s, 2)
    zp = lax.rem(z, 2)
    p = 2 * x + c
    half = lax.div(x, 2)
    rows = GROUPS * (pc + qc)

    def m4(v):
        return lax.rem(v + 8, 4)

    def dev(dx, dy, dz, dc):
        return (4 * lax.div(dz, 2) + dy, 8 * lax.rem(dz, 2) + 2 * dx + dc)

    outer = (z == 0) | (z == 3)
    inner = jnp.logical_not(outer)
    home_core = c == zp
    owner = outer & home_core
    mid = inner & home_core
    relay = outer & jnp.logical_not(home_core)
    inner_i = jnp.where(inner, 1, 0)
    za = 3 * (1 - zp)
    zb = 1 + zp
    kk = jnp.where(z < 2, 1, 0)
    own_slot = jnp.where(outer, 2 * y + (1 - kk), 8)

    k_copy = pltpu.make_async_copy(kernel_ref, kv, k_sem)
    r_copy = pltpu.make_async_copy(rates_ref, rv, r_sem)
    r_copy.start()
    k_copy.start()

    bar = pltpu.get_barrier_semaphore()
    zx = z + 1 - 2 * zp
    friends = [dev(x, m4(y + 2), z, c)]
    friends += [dev(m4(x + d), y, zx, c) for d in (2, 1, 3)]
    friends += [dev(m4(x + d), y, z, 1 - c if k else c) for d in (2, 1, 3, 0) for k in range(2) if d or k]
    friends += [dev(x, m4(y + 1), z, c), dev(x, m4(y - 1), z, c), dev(x, y, m4(z + 1), c), dev(x, y, m4(z - 1), c)]
    gives_own = (r == 0) & (s < 8)

    @pl.when(jnp.logical_not((r == 0) & (s == 0)))
    def _():
        pl.semaphore_signal(bar, inc=1, device_id=(0, r), device_id_type=MESH)

    for f in friends:
        pl.semaphore_signal(bar, inc=1, device_id=f, device_id_type=MESH)

    r_copy.wait()

    def cols(t):
        return slice(LANES * (t // GROUPS), LANES * (t // GROUPS + 1))

    for t in range(CHUNKS):
        j = t % GROUPS
        qbuf[t, y] = (rv[GROUPS * pc + j * qc:GROUPS * pc + (j + 1) * qc, cols(t)] - 1.0).astype(jnp.bfloat16)
        pbuf[t, own_slot] = (rv[j * pc:(j + 1) * pc, cols(t)] - 1.0).astype(jnp.bfloat16)

    pl.semaphore_wait(bar, len(friends) + jnp.where(gives_own, jnp.where(s == 0, 15, 16), 0))

    def remote(src, dst, ssem, rsem, to):
        return pltpu.make_async_remote_copy(
            src_ref=src, dst_ref=dst, send_sem=ssem, recv_sem=rsem, device_id=to, device_id_type=MESH
        )

    def landed(dst, sem):
        pltpu.make_async_copy(dst, dst, sem).wait()

    def send_pa(t):
        dst = jnp.where(outer, 8, 2 * y + kk)
        sem = jnp.where(outer, 2, kk)
        remote(pbuf.at[t, own_slot], pbuf.at[t, dst], pa_s, pz_r.at[t, sem], dev(x, y, za, c)).start()

    def send_pb(t):
        remote(pbuf.at[t, 8], pbuf.at[t, 2 * y + kk], pb_s, pz_r.at[t, kk], dev(x, y, zb, c)).start()

    def p_relay(t):
        @pl.when(outer)
        def _():
            landed(pbuf.at[t, 8], pz_r.at[t, 2])
            send_pb(t)

    def p_slots(t):
        landed(pbuf.at[t, 2 * y + kk], pz_r.at[t, kk])

        @pl.when(inner)
        def _():
            landed(pbuf.at[t, 2 * y + 1 - kk], pz_r.at[t, 1 - kk])

        part = pbuf.at[t, pl.ds(2 * y, 2)]
        for d in (2, 1, 3):
            remote(part, part, py_s, py_r.at[t, d - 1], dev(x, m4(y + d), z, c)).start()

    def send_px(t, e):
        to_x = m4(y + e)
        dst = dp.at[t, p]
        for k in range(2):
            core = 1 - c if k else c
            src = pbuf.at[t, 2 * to_x + core]
            there = remote(src, dst, px_s, px_r.at[t], dev(to_x, y, z, core))
            if k:
                there.start()
            else:
                pl.when(to_x != x)(there.start)
                here = pltpu.make_async_copy(src, dst, px_r.at[t])
                pl.when(to_x == x)(here.start)

    def p_x(t):
        send_px(t, 0)
        for d in (1, 3, 2):
            landed(pbuf.at[t, pl.ds(2 * m4(y - d), 2)], py_r.at[t, d - 1])
            send_px(t, 4 - d)

    def send_qy(t):
        part = qbuf.at[t, y]
        for d in (2, 1, 3):
            remote(part, part, qy_s, qy_r.at[t, d - 1], dev(x, m4(y + d), z, c)).start()

    def send_qx(t, e):
        to_x = m4(y + e)
        src = qbuf.at[t, to_x]
        dst = dq.at[inner_i, t, p]
        sem = d_r.at[inner_i, t, half]
        me = (to_x == x) & home_core
        there = remote(src, dst, qx_s, sem, dev(to_x, y, z, zp))
        here = pltpu.make_async_copy(src, dst, sem)
        pl.when(jnp.logical_not(me))(there.start)
        pl.when(me)(here.start)

    def q_x(t):
        for d in (1, 3, 2):
            landed(qbuf.at[t, m4(y - d)], qy_r.at[t, d - 1])
            send_qx(t, 4 - d)

    def q_z(t):
        for g in range(2):
            final = dq.at[0, t, pl.ds(4 * g, 4)]
            spare = dq.at[1, t, pl.ds(4 * g, 4)]
            f_sem = d_r.at[0, t, g]
            s_sem = d_r.at[1, t, g]

            @pl.when(owner)
            def _():
                landed(final, f_sem)
                remote(final, spare, qa_s, s_sem, dev(x, y, za, c)).start()

            @pl.when(mid)
            def _():
                landed(spare, s_sem)
                remote(spare, final, qa_s, f_sem, dev(x, y, za, c)).start()
                remote(spare, final, qb_s, f_sem, dev(x, y, zb, c)).start()

    def q_relay(t):
        for g in range(2):
            final = dq.at[0, t, pl.ds(4 * g, 4)]
            spare = dq.at[1, t, pl.ds(4 * g, 4)]

            @pl.when(relay)
            def _():
                landed(spare, d_r.at[1, t, g])
                remote(spare, final, qb_s, d_r.at[0, t, g], dev(x, y, zb, c)).start()

    def regroup(j):
        @pl.loop(0, rows // 96)
        def _(i):
            at = pl.ds(pl.multiple_of(i * 96, 96), 96)
            for n in range(8):
                a = n * rows + j * pc
                kp[j, at, n * pc:(n + 1) * pc] = kv[at, a:a + pc]
                a = n * rows + GROUPS * pc + j * qc
                kq[j, at, n * qc:(n + 1) * qc] = kv[at, a:a + qc]

    def product(t):
        j = t % GROUPS
        landed(dp.at[t], px_r.at[t])
        part = jnp.dot(kp[j], dp[t].reshape(8 * pc, LANES), preferred_element_type=jnp.float32)
        if j == 0:
            acc[...] = part
        else:
            acc[...] += part

        @pl.when(jnp.logical_not(owner))
        def _():
            for g in range(2):
                landed(dq.at[0, t, pl.ds(4 * g, 4)], d_r.at[0, t, g])

        acc[...] += jnp.dot(kq[j], dq[0, t].reshape(8 * qc, LANES), preferred_element_type=jnp.float32)

    rec = rows // 16

    def sum_start(h):
        for b in range(16):
            sb[h, b % 2, b // 2, :rec] = acc[b * rec:(b + 1) * rec]
        remote(sb.at[h, 1 - c], cb.at[h], cx_s.at[h], cx_r.at[h], dev(x, y, z, 1 - c)).start()

    def sum_cores(h):
        landed(cb.at[h], cx_r.at[h])
        sb[h, c] = sb[h, c] + cb[h]
        for n in (6, 5, 7, 2, 1, 3, 4):
            to_x = m4(x + n % 4)
            to_z = zx if n >= 4 else z
            block = 4 * lax.rem(to_z, 2) + to_x
            remote(sb.at[h, c, block], rb.at[h, n], rs_s.at[h], rs_r.at[h, n], dev(to_x, y, to_z, c)).start()

    def sum_end(h):
        total = sb[h, c, 4 * zp + x]
        for n in range(1, 8):
            landed(rb.at[h, n], rs_r.at[h, n])
            total = total + rb[h, n]
        stress_ref[:, LANES * h:LANES * (h + 1)] = total[:rec]

    for t in range(CHUNKS):
        send_qy(t)
        send_pa(t)
        pl.when(inner)(functools.partial(send_pb, t))
    for t in range(CHUNKS):
        send_qx(t, 0)

    @pl.when(gives_own)
    def _():
        for b in range(16):
            ob[b, :rec] = (rv[b * rec:(b + 1) * rec] - 1.0).astype(jnp.bfloat16)
            there = remote(ob.at[b], od, od_s, od_r, (s, b))
            if b:
                there.start()
            else:
                pl.when(s != 0)(there.start)
                pl.when(s == 0)(pltpu.make_async_copy(ob.at[b], od, od_r).start)

    k_copy.wait()
    p_relay(0)
    p_relay(1)
    p_relay(2)
    q_x(0)
    p_relay(3)
    p_slots(0)
    p_relay(4)
    p_slots(1)
    q_x(1)
    p_relay(5)
    p_slots(2)
    p_slots(3)
    regroup(0)
    q_x(2)
    p_slots(4)
    q_z(0)
    p_slots(5)
    q_x(3)
    q_z(1)
    regroup(1)
    q_x(4)
    q_z(2)
    q_x(5)
    q_z(3)
    q_relay(0)
    regroup(2)
    q_z(4)
    p_x(0)
    q_z(5)
    q_relay(1)
    p_x(1)
    q_relay(2)
    p_x(2)
    product(0)
    q_relay(3)
    p_x(3)
    product(1)
    p_x(4)
    q_relay(4)
    product(2)
    sum_start(0)
    p_x(5)
    q_relay(5)
    sum_cores(0)
    product(3)
    product(4)
    sum_end(0)
    product(5)
    sum_start(1)
    sum_cores(1)
    landed(od, od_r)
    own_ref[...] = od[:rec].astype(jnp.float32)
    sum_end(1)

    def sent(sem, like):
        pltpu.make_async_copy(like, like, sem).wait()

    sent(pa_s, pbuf.at[:, 0])
    sent(pb_s, pbuf.at[:, 0])
    sent(py_s, pbuf.at[:, pl.ds(0, 6)])
    sent(px_s, pbuf.at[:, pl.ds(0, 7)])
    sent(qy_s, qbuf.at[:, pl.ds(0, 3)])

    @pl.when(home_core)
    def _():
        sent(qx_s, qbuf.at[:, pl.ds(0, 3)])
        sent(qa_s, dq.at[0])

    @pl.when(jnp.logical_not(home_core))
    def _():
        sent(qx_s, qbuf)

    @pl.when(mid | relay)
    def _():
        sent(qb_s, dq.at[0])

    for h in range(2):
        sent(cx_s.at[h], sb.at[h, 0])
        sent(rs_s.at[h], sb.at[h, 0, pl.ds(0, 7)])

    @pl.when(gives_own & (s != 0))
    def _():
        sent(od_s, ob)

    @pl.when(gives_own & (s == 0))
    def _():
        sent(od_s, ob.at[pl.ds(0, 15)])


def per_device(kernel, rates, state, a_sigma, b_sigma, slip_distance):
    patches, members = rates.shape
    rec_rows = state.shape[0]
    pc, qc = 128, 160
    bf16, f32 = jnp.bfloat16, jnp.float32
    dma = pltpu.SemaphoreType.DMA
    rec_pad = -(-rec_rows // 8) * 8
    stress, own_deficit = pl.pallas_call(
        functools.partial(gather_and_multiply, pc, qc),
        out_shape=[jax.ShapeDtypeStruct((rec_rows, members), f32)] * 2,
        in_specs=[pl.BlockSpec(memory_space=pl.ANY)] * 2,
        out_specs=[pl.BlockSpec(memory_space=pltpu.VMEM)] * 2,
        scratch_shapes=[
            pltpu.VMEM(kernel.shape, bf16),
            pltpu.VMEM((GROUPS, patches, 8 * pc), bf16),
            pltpu.VMEM((GROUPS, patches, 8 * qc), bf16),
            pltpu.VMEM(rates.shape, f32),
            pltpu.VMEM((CHUNKS, 9, pc, LANES), bf16),
            pltpu.VMEM((CHUNKS, 4, qc, LANES), bf16),
            pltpu.VMEM((CHUNKS, 8, pc, LANES), bf16),
            pltpu.VMEM((2, CHUNKS, 8, qc, LANES), bf16),
            pltpu.VMEM((patches, LANES), f32),
            pltpu.VMEM((2, 2, 8, rec_pad, LANES), f32),
            pltpu.VMEM((2, 8, rec_pad, LANES), f32),
            pltpu.VMEM((2, 8, rec_pad, LANES), f32),
            pltpu.VMEM((16, 64, members), bf16),
            pltpu.VMEM((64, members), bf16),
            dma, dma,
            dma((CHUNKS, 3)), dma((CHUNKS, 3)), dma((CHUNKS,)), dma((CHUNKS, 3)), dma((2, CHUNKS, 2)),
            dma((2, 8)), dma((2,)), dma,
            dma, dma, dma, dma, dma, dma, dma, dma, dma((2,)), dma((2,)), dma,
        ],
        compiler_params=pltpu.CompilerParams(
            collective_id=0, has_side_effects=True, vmem_limit_bytes=60 * 2**20
        ),
        cost_estimate=pl.CostEstimate(
            flops=2 * kernel.size * members, bytes_accessed=kernel.size * 2 + rates.size * 4, transcendentals=0
        ),
    )(kernel, rates)
    own_rate = own_deficit + 1.0
    state_change = 1.0 - own_rate * state / slip_distance
    rate_change = (stress - b_sigma / state * state_change) / (a_sigma / own_rate + damping)
    return (rate_change, state_change)


def solution(mesh):
    rows = P(("rcv", "src"), None)
    return jax.shard_map(
        per_device, mesh=mesh, in_specs=(P("rcv", "src"), rows, rows, rows, rows, rows),
        out_specs=(rows, rows), check_vma=False,
    )
```

```python
import functools

import jax
import jax.numpy as jnp
from jax import lax
from jax.experimental import pallas as pl
from jax.experimental.pallas import tpu as pltpu
from jax.sharding import PartitionSpec as P

damping = 0.5
MESH = pl.DeviceIdType.MESH
LANES = 128
P_GROUPS = (128, 128, 128)
Q_GROUPS = (160, 160, 160)
P_CHUNKS = ((0, 0), (0, 1), (0, 2), (1, 0), (1, 1), (1, 2))
Q_CHUNKS = ((0, 0), (0, 1), (0, 2), (1, 0), (1, 1), (1, 2))


def gather_and_multiply(
    kernel_ref, rates_ref, stress_ref, own_ref,
    kv, rv, pbuf, qbuf, acc, sb, cb, tb, rb, ob, od, op,
    k_sem, r_sem, pz_r, py_r, px_r, qy_r, d_r, rs_r, cx_r, od_r, op_r,
    pa_s, pb_s, py_s, px_s, qy_s, qx_s, qa_s, qb_s, cx_s, rs_s, od_s, op_s,
    *grouped,
):
    np_, nq_ = len(P_GROUPS), len(Q_GROUPS)
    kp, grouped = grouped[:np_], grouped[np_:]
    kq, grouped = grouped[:nq_], grouped[nq_:]
    dp, dq = grouped[:np_], grouped[np_:]
    p_rows = sum(P_GROUPS)
    p_at = [sum(P_GROUPS[:j]) for j in range(np_)]
    q_at = [sum(Q_GROUPS[:j]) for j in range(nq_)]
    r = lax.axis_index("rcv")
    s = lax.axis_index("src")
    y = lax.rem(r, 4)
    z = 2 * lax.div(r, 4) + lax.div(s, 8)
    x = lax.div(lax.rem(s, 8), 2)
    c = lax.rem(s, 2)
    zp = lax.rem(z, 2)
    p = 2 * x + c
    half = lax.div(x, 2)
    rows = p_rows + sum(Q_GROUPS)

    def m4(v):
        return lax.rem(v + 8, 4)

    def dev(dx, dy, dz, dc):
        return (4 * lax.div(dz, 2) + dy, 8 * lax.rem(dz, 2) + 2 * dx + dc)

    outer = (z == 0) | (z == 3)
    inner = jnp.logical_not(outer)
    home_core = c == zp
    owner = outer & home_core
    mid = inner & home_core
    relay = outer & jnp.logical_not(home_core)
    inner_i = jnp.where(inner, 1, 0)
    za = 3 * (1 - zp)
    zb = 1 + zp
    kk = jnp.where(z < 2, 1, 0)
    own_slot = jnp.where(outer, 2 * y + (1 - kk), 8)

    k_copy = pltpu.make_async_copy(kernel_ref, kv, k_sem)
    r_copy = pltpu.make_async_copy(rates_ref, rv, r_sem)
    r_copy.start()
    k_copy.start()

    bar = pltpu.get_barrier_semaphore()
    zx = z + 1 - 2 * zp
    friends = [dev(x, m4(y + 2), z, c)]
    friends += [dev(m4(x + d), y, zx, c) for d in (2, 1, 3)]
    friends += [dev(m4(x + d), y, z, 1 - c if k else c) for d in (2, 1, 3, 0) for k in range(2) if d or k]
    friends += [dev(x, m4(y + 1), z, c), dev(x, m4(y - 1), z, c), dev(x, y, m4(z + 1), c), dev(x, y, m4(z - 1), c)]
    gives_own = (s < 8) & (r == lax.rem(s, 4))
    in_own = s < 4

    @pl.when(jnp.logical_not((r < 4) & (s == r)))
    def _():
        pl.semaphore_signal(bar, inc=1, device_id=(lax.rem(r, 4), r), device_id_type=MESH)

    for f in friends:
        pl.semaphore_signal(bar, inc=1, device_id=f, device_id_type=MESH)

    r_copy.wait()

    for h in range(2):
        cols = slice(LANES * h, LANES * (h + 1))
        qbuf[h, y] = (rv[p_rows:, cols] - 1.0).astype(jnp.bfloat16)
        pbuf[h, own_slot] = (rv[:p_rows, cols] - 1.0).astype(jnp.bfloat16)

    pl.semaphore_wait(bar, len(friends) + jnp.where(gives_own, jnp.where(in_own, 15, 16), 0))

    def remote(src, dst, ssem, rsem, to):
        return pltpu.make_async_remote_copy(
            src_ref=src, dst_ref=dst, send_sem=ssem, recv_sem=rsem, device_id=to, device_id_type=MESH
        )

    def landed(dst, sem):
        pltpu.make_async_copy(dst, dst, sem).wait()

    def p_part(t, slot, n=None):
        h, j = P_CHUNKS[t]
        part = pl.ds(p_at[j], P_GROUPS[j])
        return pbuf.at[h, slot, part] if n is None else pbuf.at[h, pl.ds(slot, n), part]

    def q_part(t, slot):
        h, j = Q_CHUNKS[t]
        return qbuf.at[h, slot, pl.ds(q_at[j], Q_GROUPS[j])]

    def send_pa(t):
        dst = jnp.where(outer, 8, 2 * y + kk)
        sem = jnp.where(outer, 2, kk)
        remote(p_part(t, own_slot), p_part(t, dst), pa_s, pz_r.at[t, sem], dev(x, y, za, c)).start()

    def send_pb(t):
        remote(p_part(t, 8), p_part(t, 2 * y + kk), pb_s, pz_r.at[t, kk], dev(x, y, zb, c)).start()

    def p_relay(t):
        @pl.when(outer)
        def _():
            landed(p_part(t, 8), pz_r.at[t, 2])
            send_pb(t)

    def p_slots(t):
        landed(p_part(t, 2 * y + kk), pz_r.at[t, kk])

        @pl.when(inner)
        def _():
            landed(p_part(t, 2 * y + 1 - kk), pz_r.at[t, 1 - kk])

        part = p_part(t, 2 * y, 2)
        for d in (2, 1, 3):
            remote(part, part, py_s, py_r.at[t, d - 1], dev(x, m4(y + d), z, c)).start()

    def send_px(t, e):
        h, j = P_CHUNKS[t]
        to_x = m4(y + e)
        dst = dp[j].at[h, p]
        for k in range(2):
            core = 1 - c if k else c
            src = p_part(t, 2 * to_x + core)
            there = remote(src, dst, px_s, px_r.at[t], dev(to_x, y, z, core))
            if k:
                there.start()
            else:
                pl.when(to_x != x)(there.start)
                here = pltpu.make_async_copy(src, dst, px_r.at[t])
                pl.when(to_x == x)(here.start)

    def p_ring(t):
        send_px(t, 0)
        for d in (1, 3):
            landed(p_part(t, 2 * m4(y - d), 2), py_r.at[t, d - 1])
            send_px(t, 4 - d)

    def p_far(t):
        landed(p_part(t, 2 * m4(y + 2), 2), py_r.at[t, 1])
        send_px(t, 2)

    def send_qy(t):
        part = q_part(t, y)
        for d in (2, 1, 3):
            remote(part, part, qy_s, qy_r.at[t, d - 1], dev(x, m4(y + d), z, c)).start()

    def send_qx(t, e):
        h, j = Q_CHUNKS[t]
        to_x = m4(y + e)
        src = q_part(t, to_x)
        dst = dq[j].at[inner_i, h, p]
        sem = d_r.at[inner_i, t, half]
        me = (to_x == x) & home_core
        there = remote(src, dst, qx_s, sem, dev(to_x, y, z, zp))
        here = pltpu.make_async_copy(src, dst, sem)
        pl.when(jnp.logical_not(me))(there.start)
        pl.when(me)(here.start)

    def q_x(t):
        for d in (1, 3, 2):
            landed(q_part(t, m4(y - d)), qy_r.at[t, d - 1])
            send_qx(t, 4 - d)

    def q_ends(t, g):
        h, j = Q_CHUNKS[t]
        return [dq[j].at[n, h, pl.ds(4 * g, 4)] for n in range(2)] + [d_r.at[n, t, g] for n in range(2)]

    def q_z(t):
        for g in range(2):
            final, spare, f_sem, s_sem = q_ends(t, g)

            @pl.when(owner)
            def _():
                landed(final, f_sem)
                remote(final, spare, qa_s, s_sem, dev(x, y, za, c)).start()

            @pl.when(mid)
            def _():
                landed(spare, s_sem)
                remote(spare, final, qa_s, f_sem, dev(x, y, za, c)).start()
                remote(spare, final, qb_s, f_sem, dev(x, y, zb, c)).start()

    def q_relay(t):
        for g in range(2):
            final, spare, f_sem, s_sem = q_ends(t, g)

            @pl.when(relay)
            def _():
                landed(spare, s_sem)
                remote(spare, final, qb_s, f_sem, dev(x, y, zb, c)).start()

    def regroup(i):
        groups, at_, to, first = (P_GROUPS, p_at, kp, 0) if i < np_ else (Q_GROUPS, q_at, kq, p_rows)
        j = i if i < np_ else i - np_

        @pl.loop(0, rows // 96)
        def _(i):
            at = pl.ds(pl.multiple_of(i * 96, 96), 96)
            for n in range(8):
                a = n * rows + first + at_[j]
                to[j][at, n * groups[j]:(n + 1) * groups[j]] = kv[at, a:a + groups[j]]

    def add(first, k, d, n):
        part = jnp.dot(k[...], d.reshape(8 * n, LANES), preferred_element_type=jnp.float32)
        acc[...] = part if first else acc[...] + part

    started = []

    def p_mul(t):
        h, j = P_CHUNKS[t]
        landed(dp[j].at[h], px_r.at[t])
        add(h not in started, kp[j], dp[j][h], P_GROUPS[j])
        started.append(h)

    def q_mul(t):
        h, j = Q_CHUNKS[t]

        @pl.when(jnp.logical_not(owner))
        def _():
            for g in range(2):
                final, _, f_sem, _ = q_ends(t, g)
                landed(final, f_sem)

        add(h not in started, kq[j], dq[j][0, h], Q_GROUPS[j])
        started.append(h)

    rec = rows // 16

    def sum_start(h):
        for b in range(16):
            sb[h, b % 2, b // 2, :rec] = acc[b * rec:(b + 1) * rec]
        remote(sb.at[h, 1 - c], cb.at[h], cx_s.at[h], cx_r.at[h], dev(x, y, z, 1 - c)).start()

    def sum_cores(h):
        landed(cb.at[h], cx_r.at[h])
        tb[h, :, :rec] = (sb[h, c, :, :rec] + cb[h, :, :rec]).astype(jnp.bfloat16)
        for n in (6, 5, 7, 2, 1, 3, 4):
            to_x = m4(x + n % 4)
            to_z = zx if n >= 4 else z
            block = 4 * lax.rem(to_z, 2) + to_x
            remote(tb.at[h, block], rb.at[h, n], rs_s.at[h], rs_r.at[h, n], dev(to_x, y, to_z, c)).start()

    def sum_end(h):
        mine = 4 * zp + x
        total = sb[h, c, mine, :rec] + cb[h, mine, :rec]
        for n in range(1, 8):
            landed(rb.at[h, n], rs_r.at[h, n])
            total = total + rb[h, n, :rec].astype(jnp.float32)
        stress_ref[:, LANES * h:LANES * (h + 1)] = total

    keeps = (r == 0) & (lax.rem(s, 4) == 0)

    @pl.when((r == 0) & (s < 8))
    def _():
        part = pbuf.at[:, own_slot]

        @pl.when(keeps)
        def _():
            pltpu.make_async_copy(part, op, op_r).start()

        @pl.when(jnp.logical_not(keeps))
        def _():
            remote(part, op, op_s, op_r, (lax.rem(s, 4), s)).start()

    def own_pass():
        @pl.when(gives_own)
        def _():
            landed(op, op_r)
            for h in range(2):
                cols = slice(LANES * h, LANES * (h + 1))
                rv[:p_rows, cols] = op[h].astype(jnp.float32)
                rv[p_rows:, cols] = qbuf[h, 0].astype(jnp.float32)
            for b in range(16):
                ob[b, :rec] = rv[b * rec:(b + 1) * rec].astype(jnp.bfloat16)
                there = remote(ob.at[b], od, od_s, od_r, (s, b))
                if b < 4:
                    pl.when(s != b)(there.start)
                    pl.when(s == b)(pltpu.make_async_copy(ob.at[b], od, od_r).start)
                else:
                    there.start()

    for t in range(len(Q_CHUNKS)):
        send_qy(t)
    for t in range(len(P_CHUNKS)):
        send_pa(t)
        pl.when(inner)(functools.partial(send_pb, t))
    for t in range(len(Q_CHUNKS)):
        send_qx(t, 0)

    k_wait = k_copy.wait
    k_wait()
    p_relay(0)
    p_relay(1)
    p_relay(2)
    q_x(0)
    p_relay(3)
    p_slots(0)
    p_relay(4)
    p_slots(1)
    q_x(1)
    p_relay(5)
    p_slots(2)
    p_slots(3)
    regroup(0)
    regroup(1)
    q_x(2)
    p_slots(4)
    q_z(0)
    p_slots(5)
    q_x(3)
    q_z(1)
    regroup(2)
    regroup(3)
    q_x(4)
    q_z(2)
    q_x(5)
    q_z(3)
    own_pass()
    q_relay(0)
    regroup(4)
    regroup(5)
    q_z(4)
    p_ring(0)
    p_far(0)
    q_z(5)
    q_relay(1)
    p_ring(1)
    p_far(1)
    q_relay(2)
    p_ring(2)
    p_far(2)
    p_mul(0)
    q_mul(0)
    q_relay(3)
    p_ring(3)
    p_far(3)
    p_mul(1)
    q_mul(1)
    p_ring(4)
    p_far(4)
    q_relay(4)
    p_mul(2)
    q_mul(2)
    sum_start(0)
    p_ring(5)
    p_far(5)
    q_relay(5)
    sum_cores(0)
    p_mul(3)
    q_mul(3)
    p_mul(4)
    q_mul(4)
    p_mul(5)
    q_mul(5)
    sum_start(1)
    sum_end(0)
    sum_cores(1)
    landed(od, od_r)
    own_ref[...] = od[:rec].astype(jnp.float32)
    sum_end(1)

    def sent(sem, like):
        pltpu.make_async_copy(like, like, sem).wait()

    sent(pa_s, pbuf.at[:, 0])
    sent(pb_s, pbuf.at[:, 0])
    sent(py_s, pbuf.at[:, pl.ds(0, 6)])
    sent(px_s, pbuf.at[:, pl.ds(0, 7)])
    sent(qy_s, qbuf.at[:, pl.ds(0, 3)])

    @pl.when(home_core)
    def _():
        sent(qx_s, qbuf.at[:, pl.ds(0, 3)])

    @pl.when(jnp.logical_not(home_core))
    def _():
        sent(qx_s, qbuf)

    for j in range(nq_):
        @pl.when(home_core)
        def _():
            sent(qa_s, dq[j].at[0])

        @pl.when(mid | relay)
        def _():
            sent(qb_s, dq[j].at[0])

    for h in range(2):
        sent(cx_s.at[h], sb.at[h, 0])
        sent(rs_s.at[h], tb.at[h, pl.ds(0, 7)])

    @pl.when((r == 0) & (s < 8) & jnp.logical_not(keeps))
    def _():
        sent(op_s, op)

    @pl.when(gives_own & in_own)
    def _():
        sent(od_s, ob.at[pl.ds(0, 15)])

    @pl.when(gives_own & jnp.logical_not(in_own))
    def _():
        sent(od_s, ob)


def per_device(kernel, rates, state, a_sigma, b_sigma, slip_distance):
    patches, members = rates.shape
    rec_rows = state.shape[0]
    p_rows, q_rows = sum(P_GROUPS), sum(Q_GROUPS)
    assert p_rows + q_rows == patches
    p_chunks, q_chunks = len(P_CHUNKS), len(Q_CHUNKS)
    bf16, f32 = jnp.bfloat16, jnp.float32
    dma = pltpu.SemaphoreType.DMA
    rec_pad = -(-rec_rows // 8) * 8
    stress, own_deficit = pl.pallas_call(
        gather_and_multiply,
        out_shape=[jax.ShapeDtypeStruct((rec_rows, members), f32)] * 2,
        in_specs=[pl.BlockSpec(memory_space=pl.ANY)] * 2,
        out_specs=[pl.BlockSpec(memory_space=pltpu.VMEM)] * 2,
        scratch_shapes=[
            pltpu.VMEM(kernel.shape, bf16),
            pltpu.VMEM(rates.shape, f32),
            pltpu.VMEM((2, 9, p_rows, LANES), bf16),
            pltpu.VMEM((2, 4, q_rows, LANES), bf16),
            pltpu.VMEM((patches, LANES), f32),
            pltpu.VMEM((2, 2, 8, rec_pad, LANES), f32),
            pltpu.VMEM((2, 8, rec_pad, LANES), f32),
            pltpu.VMEM((2, 8, 64, LANES), bf16),
            pltpu.VMEM((2, 8, 64, LANES), bf16),
            pltpu.VMEM((16, 64, members), bf16),
            pltpu.VMEM((64, members), bf16),
            pltpu.VMEM((2, p_rows, LANES), bf16),
            dma, dma,
            dma((p_chunks, 3)), dma((p_chunks, 3)), dma((p_chunks,)),
            dma((q_chunks, 3)), dma((2, q_chunks, 2)),
            dma((2, 8)), dma((2,)), dma, dma,
            dma, dma, dma, dma, dma, dma, dma, dma, dma((2,)), dma((2,)), dma, dma,
            *[pltpu.VMEM((patches, 8 * n), bf16) for n in P_GROUPS],
            *[pltpu.VMEM((patches, 8 * n), bf16) for n in Q_GROUPS],
            *[pltpu.VMEM((2, 8, n, LANES), bf16) for n in P_GROUPS],
            *[pltpu.VMEM((2, 2, 8, n, LANES), bf16) for n in Q_GROUPS],
        ],
        compiler_params=pltpu.CompilerParams(
            collective_id=0, has_side_effects=True, vmem_limit_bytes=60 * 2**20
        ),
        cost_estimate=pl.CostEstimate(
            flops=2 * kernel.size * members, bytes_accessed=kernel.size * 2 + rates.size * 4, transcendentals=0
        ),
    )(kernel, rates)
    own_rate = own_deficit + 1.0
    state_change = 1.0 - own_rate * state / slip_distance
    rate_change = (stress - b_sigma / state * state_change) / (a_sigma / own_rate + damping)
    return (rate_change, state_change)


def solution(mesh):
    rows = P(("rcv", "src"), None)
    return jax.shard_map(
        per_device, mesh=mesh, in_specs=(P("rcv", "src"), rows, rows, rows, rows, rows),
        out_specs=(rows, rows), check_vma=False,
    )
```

```python
import functools

import jax
import jax.numpy as jnp
from jax import lax
from jax.experimental import pallas as pl
from jax.experimental.pallas import tpu as pltpu
from jax.sharding import PartitionSpec as P

damping = 0.5
MESH = pl.DeviceIdType.MESH
LANES = 128
P_GROUPS = (96, 144, 144)
Q_GROUPS = (128, 176, 176)
P_CHUNKS = ((0, 0), (0, 1), (0, 2), (1, 1), (1, 2), (1, 0))
Q_CHUNKS = ((0, 0), (0, 1), (0, 2), (1, 1), (1, 2), (1, 0))


def gather_and_multiply(
    kernel_ref, rates_ref, stress_ref, own_ref,
    kv, rv, pbuf, qbuf, acc, sb, cb, tb, rb, ob, od, op,
    k_sem, r_sem, pz_r, py_r, px_r, qy_r, d_r, rs_r, cx_r, od_r, op_r,
    pa_s, pb_s, py_s, px_s, qy_s, qx_s, qa_s, qb_s, cx_s, rs_s, od_s, op_s,
    *grouped,
):
    np_, nq_ = len(P_GROUPS), len(Q_GROUPS)
    kp, grouped = grouped[:np_], grouped[np_:]
    kq, grouped = grouped[:nq_], grouped[nq_:]
    dp, dq = grouped[:np_], grouped[np_:]
    p_rows = sum(P_GROUPS)
    p_at = [sum(P_GROUPS[:j]) for j in range(np_)]
    q_at = [sum(Q_GROUPS[:j]) for j in range(nq_)]
    r = lax.axis_index("rcv")
    s = lax.axis_index("src")
    y = lax.rem(r, 4)
    z = 2 * lax.div(r, 4) + lax.div(s, 8)
    x = lax.div(lax.rem(s, 8), 2)
    c = lax.rem(s, 2)
    zp = lax.rem(z, 2)
    p = 2 * x + c
    half = lax.div(x, 2)
    rows = p_rows + sum(Q_GROUPS)

    def m4(v):
        return lax.rem(v + 8, 4)

    def dev(dx, dy, dz, dc):
        return (4 * lax.div(dz, 2) + dy, 8 * lax.rem(dz, 2) + 2 * dx + dc)

    outer = (z == 0) | (z == 3)
    inner = jnp.logical_not(outer)
    home_core = c == zp
    owner = outer & home_core
    mid = inner & home_core
    relay = outer & jnp.logical_not(home_core)
    inner_i = jnp.where(inner, 1, 0)
    za = 3 * (1 - zp)
    zb = 1 + zp
    kk = jnp.where(z < 2, 1, 0)
    own_slot = jnp.where(outer, 2 * y + (1 - kk), 8)

    k_copy = pltpu.make_async_copy(kernel_ref, kv, k_sem)
    r_copy = pltpu.make_async_copy(rates_ref, rv, r_sem)
    r_copy.start()
    k_copy.start()

    bar = pltpu.get_barrier_semaphore()
    zx = z + 1 - 2 * zp
    friends = [dev(x, m4(y + 2), z, c)]
    friends += [dev(m4(x + d), y, zx, c) for d in (2, 1, 3)]
    friends += [dev(m4(x + d), y, z, 1 - c if k else c) for d in (2, 1, 3, 0) for k in range(2) if d or k]
    friends += [dev(x, m4(y + 1), z, c), dev(x, m4(y - 1), z, c), dev(x, y, m4(z + 1), c), dev(x, y, m4(z - 1), c)]
    gives_own = (s < 8) & (r == lax.rem(s, 4))
    in_own = s < 4

    @pl.when(jnp.logical_not((r < 4) & (s == r)))
    def _():
        pl.semaphore_signal(bar, inc=1, device_id=(lax.rem(r, 4), r), device_id_type=MESH)

    for f in friends:
        pl.semaphore_signal(bar, inc=1, device_id=f, device_id_type=MESH)

    r_copy.wait()

    for h in range(2):
        cols = slice(LANES * h, LANES * (h + 1))
        qbuf[h, y] = (rv[p_rows:, cols] - 1.0).astype(jnp.bfloat16)
        pbuf[h, own_slot] = (rv[:p_rows, cols] - 1.0).astype(jnp.bfloat16)

    pl.semaphore_wait(bar, len(friends) + jnp.where(gives_own, jnp.where(in_own, 15, 16), 0))

    def remote(src, dst, ssem, rsem, to):
        return pltpu.make_async_remote_copy(
            src_ref=src, dst_ref=dst, send_sem=ssem, recv_sem=rsem, device_id=to, device_id_type=MESH
        )

    def landed(dst, sem):
        pltpu.make_async_copy(dst, dst, sem).wait()

    def p_part(t, slot, n=None):
        h, j = P_CHUNKS[t]
        part = pl.ds(p_at[j], P_GROUPS[j])
        return pbuf.at[h, slot, part] if n is None else pbuf.at[h, pl.ds(slot, n), part]

    def q_part(t, slot):
        h, j = Q_CHUNKS[t]
        return qbuf.at[h, slot, pl.ds(q_at[j], Q_GROUPS[j])]

    def send_pa(t):
        dst = jnp.where(outer, 8, 2 * y + kk)
        sem = jnp.where(outer, 2, kk)
        remote(p_part(t, own_slot), p_part(t, dst), pa_s, pz_r.at[t, sem], dev(x, y, za, c)).start()

    def send_pb(t):
        remote(p_part(t, 8), p_part(t, 2 * y + kk), pb_s, pz_r.at[t, kk], dev(x, y, zb, c)).start()

    def p_relay(t):
        @pl.when(outer)
        def _():
            landed(p_part(t, 8), pz_r.at[t, 2])
            send_pb(t)

    def p_slots(t):
        landed(p_part(t, 2 * y + kk), pz_r.at[t, kk])

        @pl.when(inner)
        def _():
            landed(p_part(t, 2 * y + 1 - kk), pz_r.at[t, 1 - kk])

        part = p_part(t, 2 * y, 2)
        for d in (1, 3, 2):
            remote(part, part, py_s, py_r.at[t, d - 1], dev(x, m4(y + d), z, c)).start()

    def send_px(t, e):
        h, j = P_CHUNKS[t]
        to_x = m4(y + e)
        dst = dp[j].at[h, p]
        for k in range(2):
            core = 1 - c if k else c
            src = p_part(t, 2 * to_x + core)
            there = remote(src, dst, px_s, px_r.at[t], dev(to_x, y, z, core))
            if k:
                there.start()
            else:
                pl.when(to_x != x)(there.start)
                here = pltpu.make_async_copy(src, dst, px_r.at[t])
                pl.when(to_x == x)(here.start)

    def p_ring(t):
        send_px(t, 0)
        for d in (1, 3):
            landed(p_part(t, 2 * m4(y - d), 2), py_r.at[t, d - 1])
            send_px(t, 4 - d)

    def p_far(t):
        landed(p_part(t, 2 * m4(y + 2), 2), py_r.at[t, 1])
        send_px(t, 2)

    def send_qy(t):
        part = q_part(t, y)
        for d in (2, 1, 3):
            remote(part, part, qy_s, qy_r.at[t, d - 1], dev(x, m4(y + d), z, c)).start()

    def send_qx(t, e):
        h, j = Q_CHUNKS[t]
        to_x = m4(y + e)
        src = q_part(t, to_x)
        dst = dq[j].at[inner_i, h, p]
        sem = d_r.at[inner_i, t, half]
        me = (to_x == x) & home_core
        there = remote(src, dst, qx_s, sem, dev(to_x, y, z, zp))
        here = pltpu.make_async_copy(src, dst, sem)
        pl.when(jnp.logical_not(me))(there.start)
        pl.when(me)(here.start)

    def q_x(t):
        for d in (1, 3, 2):
            landed(q_part(t, m4(y - d)), qy_r.at[t, d - 1])
            send_qx(t, 4 - d)

    def q_ends(t, g):
        h, j = Q_CHUNKS[t]
        return [dq[j].at[n, h, pl.ds(4 * g, 4)] for n in range(2)] + [d_r.at[n, t, g] for n in range(2)]

    def q_z(t):
        for g in range(2):
            final, spare, f_sem, s_sem = q_ends(t, g)

            @pl.when(owner)
            def _():
                landed(final, f_sem)
                remote(final, spare, qa_s, s_sem, dev(x, y, za, c)).start()

            @pl.when(mid)
            def _():
                landed(spare, s_sem)
                remote(spare, final, qa_s, f_sem, dev(x, y, za, c)).start()
                remote(spare, final, qb_s, f_sem, dev(x, y, zb, c)).start()

    def q_relay(t):
        for g in range(2):
            final, spare, f_sem, s_sem = q_ends(t, g)

            @pl.when(relay)
            def _():
                landed(spare, s_sem)
                remote(spare, final, qb_s, f_sem, dev(x, y, zb, c)).start()

    def regroup(i):
        groups, at_, to, first = (P_GROUPS, p_at, kp, 0) if i < np_ else (Q_GROUPS, q_at, kq, p_rows)
        j = i if i < np_ else i - np_

        @pl.loop(0, rows // 96)
        def _(i):
            at = pl.ds(pl.multiple_of(i * 96, 96), 96)
            for n in range(8):
                a = n * rows + first + at_[j]
                to[j][at, n * groups[j]:(n + 1) * groups[j]] = kv[at, a:a + groups[j]]

    def add(first, k, d, n):
        part = jnp.dot(k[...], d.reshape(8 * n, LANES), preferred_element_type=jnp.float32)
        acc[...] = part if first else acc[...] + part

    started = []

    def p_mul(t):
        h, j = P_CHUNKS[t]
        landed(dp[j].at[h], px_r.at[t])
        add(h not in started, kp[j], dp[j][h], P_GROUPS[j])
        started.append(h)

    def q_mul(t):
        h, j = Q_CHUNKS[t]

        @pl.when(jnp.logical_not(owner))
        def _():
            for g in range(2):
                final, _, f_sem, _ = q_ends(t, g)
                landed(final, f_sem)

        add(h not in started, kq[j], dq[j][0, h], Q_GROUPS[j])
        started.append(h)

    rec = rows // 16

    def sum_start(h):
        for b in range(16):
            sb[h, b % 2, b // 2, :rec] = acc[b * rec:(b + 1) * rec]
        remote(sb.at[h, 1 - c], cb.at[h], cx_s.at[h], cx_r.at[h], dev(x, y, z, 1 - c)).start()

    def sum_cores(h):
        landed(cb.at[h], cx_r.at[h])
        tb[h, :, :rec] = (sb[h, c, :, :rec] + cb[h, :, :rec]).astype(jnp.bfloat16)
        for n in (6, 5, 7, 2, 1, 3, 4):
            to_x = m4(x + n % 4)
            to_z = zx if n >= 4 else z
            block = 4 * lax.rem(to_z, 2) + to_x
            remote(tb.at[h, block], rb.at[h, n], rs_s.at[h], rs_r.at[h, n], dev(to_x, y, to_z, c)).start()

    def sum_end(h):
        mine = 4 * zp + x
        total = sb[h, c, mine, :rec] + cb[h, mine, :rec]
        for n in range(1, 8):
            landed(rb.at[h, n], rs_r.at[h, n])
            total = total + rb[h, n, :rec].astype(jnp.float32)
        stress_ref[:, LANES * h:LANES * (h + 1)] = total

    keeps = (r == 0) & (lax.rem(s, 4) == 0)

    @pl.when((r == 0) & (s < 8))
    def _():
        part = pbuf.at[:, own_slot]

        @pl.when(keeps)
        def _():
            pltpu.make_async_copy(part, op, op_r).start()

        @pl.when(jnp.logical_not(keeps))
        def _():
            remote(part, op, op_s, op_r, (lax.rem(s, 4), s)).start()

    def own_pass():
        @pl.when(gives_own)
        def _():
            landed(op, op_r)
            for h in range(2):
                cols = slice(LANES * h, LANES * (h + 1))
                rv[:p_rows, cols] = op[h].astype(jnp.float32)
                rv[p_rows:, cols] = qbuf[h, 0].astype(jnp.float32)
            for b in range(16):
                ob[b, :rec] = rv[b * rec:(b + 1) * rec].astype(jnp.bfloat16)
                there = remote(ob.at[b], od, od_s, od_r, (s, b))
                if b < 4:
                    pl.when(s != b)(there.start)
                    pl.when(s == b)(pltpu.make_async_copy(ob.at[b], od, od_r).start)
                else:
                    there.start()

    for t in range(len(Q_CHUNKS)):
        send_qy(t)
    for t in range(len(P_CHUNKS)):
        send_pa(t)
        pl.when(inner)(functools.partial(send_pb, t))
    for t in range(len(Q_CHUNKS)):
        send_qx(t, 0)

    k_wait = k_copy.wait
    k_wait()
    p_relay(0)
    p_relay(1)
    p_relay(2)
    q_x(0)
    p_relay(3)
    p_slots(0)
    p_relay(4)
    p_slots(1)
    q_x(1)
    p_relay(5)
    p_slots(2)
    p_slots(3)
    regroup(0)
    regroup(1)
    q_x(2)
    p_slots(4)
    q_z(0)
    p_slots(5)
    q_x(3)
    q_z(1)
    regroup(2)
    regroup(3)
    q_x(4)
    q_z(2)
    q_x(5)
    q_z(3)
    own_pass()
    q_relay(0)
    regroup(4)
    regroup(5)
    q_z(4)
    q_relay(1)
    p_ring(0)
    p_far(0)
    q_z(5)
    p_ring(1)
    p_far(1)
    q_relay(2)
    p_ring(2)
    p_far(2)
    q_mul(0)
    q_relay(3)
    p_mul(0)
    p_ring(3)
    p_far(3)
    p_mul(1)
    q_mul(1)
    p_ring(4)
    p_far(4)
    q_relay(4)
    p_mul(2)
    q_mul(2)
    sum_start(0)
    p_ring(5)
    p_far(5)
    q_relay(5)
    sum_cores(0)
    p_mul(3)
    q_mul(3)
    p_mul(4)
    q_mul(4)
    p_mul(5)
    q_mul(5)
    sum_start(1)
    sum_end(0)
    sum_cores(1)
    landed(od, od_r)
    own_ref[...] = od[:rec].astype(jnp.float32)
    sum_end(1)

    def sent(sem, like):
        pltpu.make_async_copy(like, like, sem).wait()

    sent(pa_s, pbuf.at[:, 0])
    sent(pb_s, pbuf.at[:, 0])
    sent(py_s, pbuf.at[:, pl.ds(0, 6)])
    sent(px_s, pbuf.at[:, pl.ds(0, 7)])
    sent(qy_s, qbuf.at[:, pl.ds(0, 3)])

    @pl.when(home_core)
    def _():
        sent(qx_s, qbuf.at[:, pl.ds(0, 3)])

    @pl.when(jnp.logical_not(home_core))
    def _():
        sent(qx_s, qbuf)

    for j in range(nq_):
        @pl.when(home_core)
        def _():
            sent(qa_s, dq[j].at[0])

        @pl.when(mid | relay)
        def _():
            sent(qb_s, dq[j].at[0])

    for h in range(2):
        sent(cx_s.at[h], sb.at[h, 0])
        sent(rs_s.at[h], tb.at[h, pl.ds(0, 7)])

    @pl.when((r == 0) & (s < 8) & jnp.logical_not(keeps))
    def _():
        sent(op_s, op)

    @pl.when(gives_own & in_own)
    def _():
        sent(od_s, ob.at[pl.ds(0, 15)])

    @pl.when(gives_own & jnp.logical_not(in_own))
    def _():
        sent(od_s, ob)


def per_device(kernel, rates, state, a_sigma, b_sigma, slip_distance):
    patches, members = rates.shape
    rec_rows = state.shape[0]
    p_rows, q_rows = sum(P_GROUPS), sum(Q_GROUPS)
    assert p_rows + q_rows == patches
    p_chunks, q_chunks = len(P_CHUNKS), len(Q_CHUNKS)
    bf16, f32 = jnp.bfloat16, jnp.float32
    dma = pltpu.SemaphoreType.DMA
    rec_pad = -(-rec_rows // 8) * 8
    stress, own_deficit = pl.pallas_call(
        gather_and_multiply,
        out_shape=[jax.ShapeDtypeStruct((rec_rows, members), f32)] * 2,
        in_specs=[pl.BlockSpec(memory_space=pl.ANY)] * 2,
        out_specs=[pl.BlockSpec(memory_space=pltpu.VMEM)] * 2,
        scratch_shapes=[
            pltpu.VMEM(kernel.shape, bf16),
            pltpu.VMEM(rates.shape, f32),
            pltpu.VMEM((2, 9, p_rows, LANES), bf16),
            pltpu.VMEM((2, 4, q_rows, LANES), bf16),
            pltpu.VMEM((patches, LANES), f32),
            pltpu.VMEM((2, 2, 8, rec_pad, LANES), f32),
            pltpu.VMEM((2, 8, rec_pad, LANES), f32),
            pltpu.VMEM((2, 8, 64, LANES), bf16),
            pltpu.VMEM((2, 8, 64, LANES), bf16),
            pltpu.VMEM((16, 64, members), bf16),
            pltpu.VMEM((64, members), bf16),
            pltpu.VMEM((2, p_rows, LANES), bf16),
            dma, dma,
            dma((p_chunks, 3)), dma((p_chunks, 3)), dma((p_chunks,)),
            dma((q_chunks, 3)), dma((2, q_chunks, 2)),
            dma((2, 8)), dma((2,)), dma, dma,
            dma, dma, dma, dma, dma, dma, dma, dma, dma((2,)), dma((2,)), dma, dma,
            *[pltpu.VMEM((patches, 8 * n), bf16) for n in P_GROUPS],
            *[pltpu.VMEM((patches, 8 * n), bf16) for n in Q_GROUPS],
            *[pltpu.VMEM((2, 8, n, LANES), bf16) for n in P_GROUPS],
            *[pltpu.VMEM((2, 2, 8, n, LANES), bf16) for n in Q_GROUPS],
        ],
        compiler_params=pltpu.CompilerParams(
            collective_id=0, has_side_effects=True, vmem_limit_bytes=60 * 2**20
        ),
        cost_estimate=pl.CostEstimate(
            flops=2 * kernel.size * members, bytes_accessed=kernel.size * 2 + rates.size * 4, transcendentals=0
        ),
    )(kernel, rates)
    own_rate = own_deficit + 1.0
    state_change = 1.0 - own_rate * state / slip_distance
    rate_change = (stress - b_sigma / state * state_change) / (a_sigma / own_rate + damping)
    return (rate_change, state_change)


def solution(mesh):
    rows = P(("rcv", "src"), None)
    return jax.shard_map(
        per_device, mesh=mesh, in_specs=(P("rcv", "src"), rows, rows, rows, rows, rows),
        out_specs=(rows, rows), check_vma=False,
    )
```

```python
import functools

import jax
import jax.numpy as jnp
from jax import lax
from jax.experimental import pallas as pl
from jax.experimental.pallas import tpu as pltpu
from jax.sharding import PartitionSpec as P

damping = 0.5
MESH = pl.DeviceIdType.MESH
LANES = 128
P_GROUPS = (96, 144, 144)
Q_GROUPS = (128, 176, 176)
P_CHUNKS = ((0, 0), (0, 1), (0, 2), (1, 1), (1, 2), (1, 0))
Q_CHUNKS = ((0, 0), (0, 1), (0, 2), (1, 1), (1, 2), (1, 0))


def gather_and_multiply(
    kernel_ref, rates_ref, stress_ref, own_ref,
    kv, rv, pbuf, qbuf, acc, sb, cb, tb, rb, ob, od, op,
    k_sem, r_sem, pz_r, py_r, px_r, qy_r, d_r, rs_r, cx_r, od_r, op_r,
    pa_s, pb_s, py_s, px_s, qy_s, qx_s, qa_s, qb_s, cx_s, rs_s, od_s, op_s,
    *grouped,
):
    np_, nq_ = len(P_GROUPS), len(Q_GROUPS)
    kp, grouped = grouped[:np_], grouped[np_:]
    kq, grouped = grouped[:nq_], grouped[nq_:]
    dp, dq = grouped[:np_], grouped[np_:]
    p_rows = sum(P_GROUPS)
    p_at = [sum(P_GROUPS[:j]) for j in range(np_)]
    q_at = [sum(Q_GROUPS[:j]) for j in range(nq_)]
    r = lax.axis_index("rcv")
    s = lax.axis_index("src")
    y = lax.rem(r, 4)
    z = 2 * lax.div(r, 4) + lax.div(s, 8)
    x = lax.div(lax.rem(s, 8), 2)
    c = lax.rem(s, 2)
    zp = lax.rem(z, 2)
    p = 2 * x + c
    half = lax.div(x, 2)
    rows = p_rows + sum(Q_GROUPS)

    def m4(v):
        return lax.rem(v + 8, 4)

    def dev(dx, dy, dz, dc):
        return (4 * lax.div(dz, 2) + dy, 8 * lax.rem(dz, 2) + 2 * dx + dc)

    outer = (z == 0) | (z == 3)
    inner = jnp.logical_not(outer)
    home_core = c == zp
    owner = outer & home_core
    mid = inner & home_core
    relay = outer & jnp.logical_not(home_core)
    inner_i = jnp.where(inner, 1, 0)
    za = 3 * (1 - zp)
    zb = 1 + zp
    kk = jnp.where(z < 2, 1, 0)
    own_slot = jnp.where(outer, 2 * y + (1 - kk), 8)

    k_copy = pltpu.make_async_copy(kernel_ref, kv, k_sem)
    r_copy = pltpu.make_async_copy(rates_ref, rv, r_sem)
    r_copy.start()
    k_copy.start()

    bar = pltpu.get_barrier_semaphore()
    zx = z + 1 - 2 * zp
    friends = [dev(x, m4(y + 2), z, c)]
    friends += [dev(m4(x + d), y, zx, c) for d in (2, 1, 3)]
    friends += [dev(m4(x + d), y, z, 1 - c if k else c) for d in (2, 1, 3, 0) for k in range(2) if d or k]
    friends += [dev(x, m4(y + 1), z, c), dev(x, m4(y - 1), z, c), dev(x, y, m4(z + 1), c), dev(x, y, m4(z - 1), c)]
    gives_own = (s < 8) & (r == lax.rem(s, 4))
    in_own = s < 4

    @pl.when(jnp.logical_not((r < 4) & (s == r)))
    def _():
        pl.semaphore_signal(bar, inc=1, device_id=(lax.rem(r, 4), r), device_id_type=MESH)

    for f in friends:
        pl.semaphore_signal(bar, inc=1, device_id=f, device_id_type=MESH)

    r_copy.wait()

    for h in range(2):
        cols = slice(LANES * h, LANES * (h + 1))
        qbuf[h, y] = (rv[p_rows:, cols] - 1.0).astype(jnp.bfloat16)
        pbuf[h, own_slot] = (rv[:p_rows, cols] - 1.0).astype(jnp.bfloat16)

    pl.semaphore_wait(bar, len(friends) + jnp.where(gives_own, jnp.where(in_own, 15, 16), 0))

    def remote(src, dst, ssem, rsem, to):
        return pltpu.make_async_remote_copy(
            src_ref=src, dst_ref=dst, send_sem=ssem, recv_sem=rsem, device_id=to, device_id_type=MESH
        )

    def landed(dst, sem):
        pltpu.make_async_copy(dst, dst, sem).wait()

    def p_part(t, slot, n=None):
        h, j = P_CHUNKS[t]
        part = pl.ds(p_at[j], P_GROUPS[j])
        return pbuf.at[h, slot, part] if n is None else pbuf.at[h, pl.ds(slot, n), part]

    def q_part(t, slot):
        h, j = Q_CHUNKS[t]
        return qbuf.at[h, slot, pl.ds(q_at[j], Q_GROUPS[j])]

    def send_pa(t):
        dst = jnp.where(outer, 8, 2 * y + kk)
        sem = jnp.where(outer, 2, kk)
        remote(p_part(t, own_slot), p_part(t, dst), pa_s, pz_r.at[t, sem], dev(x, y, za, c)).start()

    def send_pb(t):
        remote(p_part(t, 8), p_part(t, 2 * y + kk), pb_s, pz_r.at[t, kk], dev(x, y, zb, c)).start()

    def p_relay(t):
        @pl.when(outer)
        def _():
            landed(p_part(t, 8), pz_r.at[t, 2])
            send_pb(t)

    def p_slots(t):
        landed(p_part(t, 2 * y + kk), pz_r.at[t, kk])

        @pl.when(inner)
        def _():
            landed(p_part(t, 2 * y + 1 - kk), pz_r.at[t, 1 - kk])

        part = p_part(t, 2 * y, 2)
        for d in (1, 3, 2):
            remote(part, part, py_s, py_r.at[t, d - 1], dev(x, m4(y + d), z, c)).start()

    def send_px(t, e):
        h, j = P_CHUNKS[t]
        to_x = m4(y + e)
        dst = dp[j].at[h, p]
        for k in range(2):
            core = 1 - c if k else c
            src = p_part(t, 2 * to_x + core)
            there = remote(src, dst, px_s, px_r.at[t], dev(to_x, y, z, core))
            if k:
                there.start()
            else:
                pl.when(to_x != x)(there.start)
                here = pltpu.make_async_copy(src, dst, px_r.at[t])
                pl.when(to_x == x)(here.start)

    def p_ring(t):
        send_px(t, 0)
        for d in (1, 3):
            landed(p_part(t, 2 * m4(y - d), 2), py_r.at[t, d - 1])
            send_px(t, 4 - d)

    def p_far(t):
        landed(p_part(t, 2 * m4(y + 2), 2), py_r.at[t, 1])
        send_px(t, 2)

    def send_qy(t):
        part = q_part(t, y)
        for d in (2, 1, 3):
            remote(part, part, qy_s, qy_r.at[t, d - 1], dev(x, m4(y + d), z, c)).start()

    def send_qx(t, e):
        h, j = Q_CHUNKS[t]
        to_x = m4(y + e)
        src = q_part(t, to_x)
        dst = dq[j].at[inner_i, h, p]
        sem = d_r.at[inner_i, t, half]
        me = (to_x == x) & home_core
        there = remote(src, dst, qx_s, sem, dev(to_x, y, z, zp))
        here = pltpu.make_async_copy(src, dst, sem)
        pl.when(jnp.logical_not(me))(there.start)
        pl.when(me)(here.start)

    def q_x(t):
        for d in (1, 3, 2):
            landed(q_part(t, m4(y - d)), qy_r.at[t, d - 1])
            send_qx(t, 4 - d)

    def q_ends(t, g):
        h, j = Q_CHUNKS[t]
        return [dq[j].at[n, h, pl.ds(4 * g, 4)] for n in range(2)] + [d_r.at[n, t, g] for n in range(2)]

    def q_z(t):
        for g in range(2):
            final, spare, f_sem, s_sem = q_ends(t, g)

            @pl.when(owner)
            def _():
                landed(final, f_sem)
                remote(final, spare, qa_s, s_sem, dev(x, y, za, c)).start()

            @pl.when(mid)
            def _():
                landed(spare, s_sem)
                remote(spare, final, qa_s, f_sem, dev(x, y, za, c)).start()
                remote(spare, final, qb_s, f_sem, dev(x, y, zb, c)).start()

    def q_relay(t):
        for g in range(2):
            final, spare, f_sem, s_sem = q_ends(t, g)

            @pl.when(relay)
            def _():
                landed(spare, s_sem)
                remote(spare, final, qb_s, f_sem, dev(x, y, zb, c)).start()

    def regroup(i):
        groups, at_, to, first = (P_GROUPS, p_at, kp, 0) if i < np_ else (Q_GROUPS, q_at, kq, p_rows)
        j = i if i < np_ else i - np_

        @pl.loop(0, rows // 96)
        def _(i):
            at = pl.ds(pl.multiple_of(i * 96, 96), 96)
            for n in range(8):
                a = n * rows + first + at_[j]
                to[j][at, n * groups[j]:(n + 1) * groups[j]] = kv[at, a:a + groups[j]]

    def add(first, k, d, n):
        part = jnp.dot(k[...], d.reshape(8 * n, LANES), preferred_element_type=jnp.float32)
        acc[...] = part if first else acc[...] + part

    started = []

    def p_mul(t):
        h, j = P_CHUNKS[t]
        landed(dp[j].at[h], px_r.at[t])
        add(h not in started, kp[j], dp[j][h], P_GROUPS[j])
        started.append(h)

    def q_mul(t):
        h, j = Q_CHUNKS[t]

        @pl.when(jnp.logical_not(owner))
        def _():
            for g in range(2):
                final, _, f_sem, _ = q_ends(t, g)
                landed(final, f_sem)

        add(h not in started, kq[j], dq[j][0, h], Q_GROUPS[j])
        started.append(h)

    rec = rows // 16

    def sum_start(h):
        for b in range(16):
            sb[h, b % 2, b // 2, :rec] = acc[b * rec:(b + 1) * rec]
        remote(sb.at[h, 1 - c], cb.at[h], cx_s.at[h], cx_r.at[h], dev(x, y, z, 1 - c)).start()

    def sum_cores(h):
        landed(cb.at[h], cx_r.at[h])
        tb[h, :, :rec] = (sb[h, c, :, :rec] + cb[h, :, :rec]).astype(jnp.bfloat16)
        for n in (6, 5, 7, 2, 1, 3, 4):
            to_x = m4(x + n % 4)
            to_z = zx if n >= 4 else z
            block = 4 * lax.rem(to_z, 2) + to_x
            remote(tb.at[h, block], rb.at[h, n], rs_s.at[h], rs_r.at[h, n], dev(to_x, y, to_z, c)).start()

    part_rows = rows // 2

    def parts():
        return [(0, 1 - zp, (6, 5, 7, 4)), (1, zp, (2, 1, 3))]

    def finish_first():
        t, u = len(P_CHUNKS) - 1, len(Q_CHUNKS) - 1
        h, j = P_CHUNKS[t]
        _, i = Q_CHUNKS[u]
        landed(dp[j].at[h], px_r.at[t])

        @pl.when(jnp.logical_not(owner))
        def _():
            for g in range(2):
                final, _, f_sem, _ = q_ends(u, g)
                landed(final, f_sem)

        p_vals = dp[j][h].reshape(8 * P_GROUPS[j], LANES)
        q_vals = dq[i][0, h].reshape(8 * Q_GROUPS[i], LANES)
        for g, lo, _ in parts():
            at = pl.ds(pl.multiple_of(lo * part_rows, 16), part_rows)
            part = acc[at]
            part += jnp.dot(kp[j][at], p_vals, preferred_element_type=jnp.float32)
            part += jnp.dot(kq[i][at], q_vals, preferred_element_type=jnp.float32)
            for b in range(8):
                sb[h, b % 2, 4 * lo + b // 2, :rec] = part[b * rec:(b + 1) * rec]
            four = pl.ds(4 * lo, 4)
            remote(sb.at[h, 1 - c, four], cb.at[h, four], cx_s.at[h], cx_r.at[1 + g], dev(x, y, z, 1 - c)).start()

    def finish_last():
        h = 1
        for g, lo, targets in parts():
            four = pl.ds(4 * lo, 4)
            landed(cb.at[h, four], cx_r.at[1 + g])
            tb[h, four, :rec] = (sb[h, c, four, :rec] + cb[h, four, :rec]).astype(jnp.bfloat16)
            for n in targets:
                to_x = m4(x + n % 4)
                block = 4 * lo + to_x
                to = dev(to_x, y, zx if n >= 4 else z, c)
                remote(tb.at[h, block], rb.at[h, n], rs_s.at[h], rs_r.at[h, n], to).start()

    def sum_end(h):
        mine = 4 * zp + x
        total = sb[h, c, mine, :rec] + cb[h, mine, :rec]
        for n in range(1, 8):
            landed(rb.at[h, n], rs_r.at[h, n])
            total = total + rb[h, n, :rec].astype(jnp.float32)
        stress_ref[:, LANES * h:LANES * (h + 1)] = total

    keeps = (r == 0) & (lax.rem(s, 4) == 0)

    @pl.when((r == 0) & (s < 8))
    def _():
        part = pbuf.at[:, own_slot]

        @pl.when(keeps)
        def _():
            pltpu.make_async_copy(part, op, op_r).start()

        @pl.when(jnp.logical_not(keeps))
        def _():
            remote(part, op, op_s, op_r, (lax.rem(s, 4), s)).start()

    def own_pass():
        @pl.when(gives_own)
        def _():
            landed(op, op_r)
            for h in range(2):
                cols = slice(LANES * h, LANES * (h + 1))
                rv[:p_rows, cols] = op[h].astype(jnp.float32)
                rv[p_rows:, cols] = qbuf[h, 0].astype(jnp.float32)
            for b in range(16):
                ob[b, :rec] = rv[b * rec:(b + 1) * rec].astype(jnp.bfloat16)
                there = remote(ob.at[b], od, od_s, od_r, (s, b))
                if b < 4:
                    pl.when(s != b)(there.start)
                    pl.when(s == b)(pltpu.make_async_copy(ob.at[b], od, od_r).start)
                else:
                    there.start()

    for t in range(len(Q_CHUNKS)):
        send_qy(t)
    for t in range(len(P_CHUNKS)):
        send_pa(t)
        pl.when(inner)(functools.partial(send_pb, t))
    for t in range(len(Q_CHUNKS)):
        send_qx(t, 0)

    k_wait = k_copy.wait
    k_wait()
    p_relay(0)
    p_relay(1)
    p_relay(2)
    q_x(0)
    p_relay(3)
    p_slots(0)
    p_relay(4)
    p_slots(1)
    q_x(1)
    p_relay(5)
    p_slots(2)
    p_slots(3)
    regroup(0)
    regroup(1)
    q_x(2)
    p_slots(4)
    q_z(0)
    p_slots(5)
    q_x(3)
    q_z(1)
    regroup(2)
    regroup(3)
    q_x(4)
    q_z(2)
    q_x(5)
    q_z(3)
    own_pass()
    q_relay(0)
    regroup(4)
    regroup(5)
    q_z(4)
    q_relay(1)
    p_ring(0)
    p_far(0)
    q_z(5)
    p_ring(1)
    p_far(1)
    q_relay(2)
    p_ring(2)
    p_far(2)
    q_mul(0)
    q_relay(3)
    p_mul(0)
    p_ring(3)
    p_far(3)
    p_mul(1)
    q_mul(1)
    p_ring(4)
    p_far(4)
    q_relay(4)
    p_mul(2)
    q_mul(2)
    sum_start(0)
    p_ring(5)
    p_far(5)
    q_relay(5)
    sum_cores(0)
    p_mul(3)
    q_mul(3)
    p_mul(4)
    q_mul(4)
    finish_first()
    sum_end(0)
    finish_last()
    landed(od, od_r)
    own_ref[...] = od[:rec].astype(jnp.float32)
    sum_end(1)

    def sent(sem, like):
        pltpu.make_async_copy(like, like, sem).wait()

    sent(pa_s, pbuf.at[:, 0])
    sent(pb_s, pbuf.at[:, 0])
    sent(py_s, pbuf.at[:, pl.ds(0, 6)])
    sent(px_s, pbuf.at[:, pl.ds(0, 7)])
    sent(qy_s, qbuf.at[:, pl.ds(0, 3)])

    @pl.when(home_core)
    def _():
        sent(qx_s, qbuf.at[:, pl.ds(0, 3)])

    @pl.when(jnp.logical_not(home_core))
    def _():
        sent(qx_s, qbuf)

    for j in range(nq_):
        @pl.when(home_core)
        def _():
            sent(qa_s, dq[j].at[0])

        @pl.when(mid | relay)
        def _():
            sent(qb_s, dq[j].at[0])

    for h in range(2):
        sent(cx_s.at[h], sb.at[h, 0])
        sent(rs_s.at[h], tb.at[h, pl.ds(0, 7)])

    @pl.when((r == 0) & (s < 8) & jnp.logical_not(keeps))
    def _():
        sent(op_s, op)

    @pl.when(gives_own & in_own)
    def _():
        sent(od_s, ob.at[pl.ds(0, 15)])

    @pl.when(gives_own & jnp.logical_not(in_own))
    def _():
        sent(od_s, ob)


def per_device(kernel, rates, state, a_sigma, b_sigma, slip_distance):
    patches, members = rates.shape
    rec_rows = state.shape[0]
    p_rows, q_rows = sum(P_GROUPS), sum(Q_GROUPS)
    assert p_rows + q_rows == patches
    p_chunks, q_chunks = len(P_CHUNKS), len(Q_CHUNKS)
    bf16, f32 = jnp.bfloat16, jnp.float32
    dma = pltpu.SemaphoreType.DMA
    rec_pad = -(-rec_rows // 8) * 8
    stress, own_deficit = pl.pallas_call(
        gather_and_multiply,
        out_shape=[jax.ShapeDtypeStruct((rec_rows, members), f32)] * 2,
        in_specs=[pl.BlockSpec(memory_space=pl.ANY)] * 2,
        out_specs=[pl.BlockSpec(memory_space=pltpu.VMEM)] * 2,
        scratch_shapes=[
            pltpu.VMEM(kernel.shape, bf16),
            pltpu.VMEM(rates.shape, f32),
            pltpu.VMEM((2, 9, p_rows, LANES), bf16),
            pltpu.VMEM((2, 4, q_rows, LANES), bf16),
            pltpu.VMEM((patches, LANES), f32),
            pltpu.VMEM((2, 2, 8, rec_pad, LANES), f32),
            pltpu.VMEM((2, 8, rec_pad, LANES), f32),
            pltpu.VMEM((2, 8, 64, LANES), bf16),
            pltpu.VMEM((2, 8, 64, LANES), bf16),
            pltpu.VMEM((16, 64, members), bf16),
            pltpu.VMEM((64, members), bf16),
            pltpu.VMEM((2, p_rows, LANES), bf16),
            dma, dma,
            dma((p_chunks, 3)), dma((p_chunks, 3)), dma((p_chunks,)),
            dma((q_chunks, 3)), dma((2, q_chunks, 2)),
            dma((2, 8)), dma((3,)), dma, dma,
            dma, dma, dma, dma, dma, dma, dma, dma, dma((2,)), dma((2,)), dma, dma,
            *[pltpu.VMEM((patches, 8 * n), bf16) for n in P_GROUPS],
            *[pltpu.VMEM((patches, 8 * n), bf16) for n in Q_GROUPS],
            *[pltpu.VMEM((2, 8, n, LANES), bf16) for n in P_GROUPS],
            *[pltpu.VMEM((2, 2, 8, n, LANES), bf16) for n in Q_GROUPS],
        ],
        compiler_params=pltpu.CompilerParams(
            collective_id=0, has_side_effects=True, vmem_limit_bytes=60 * 2**20
        ),
        cost_estimate=pl.CostEstimate(
            flops=2 * kernel.size * members, bytes_accessed=kernel.size * 2 + rates.size * 4, transcendentals=0
        ),
    )(kernel, rates)
    own_rate = own_deficit + 1.0
    state_change = 1.0 - own_rate * state / slip_distance
    rate_change = (stress - b_sigma / state * state_change) / (a_sigma / own_rate + damping)
    return (rate_change, state_change)


def solution(mesh):
    rows = P(("rcv", "src"), None)
    return jax.shard_map(
        per_device, mesh=mesh, in_specs=(P("rcv", "src"), rows, rows, rows, rows, rows),
        out_specs=(rows, rows), check_vma=False,
    )
```
